32 devices in a mesh: row: 8 (over z, core), col: 4 (over y, x).
Axes of the slice: x: 2, y: 2, z: 4, core: 2. Of those that a mesh axis runs over, the one named last changes fastest.
Arguments:
- matrix: float32 [16, 8, 128, 32, 4, 128], P(None, 'row', None, None, 'col'), as said below
Outputs:
- swept: float32 [16, 8, 128, 32, 4, 128], P(None, 'row', None, None, 'col')
Inputs may be any that keep to these rules, and one draw needn't show every extreme that they name: `matrix`: every diagonal entry is at least sqrt(16384) - 6 and every off-diagonal entry has magnitude at most 6.
All inputs are finite; a program needn't handle non-finite values.
Results may differ from the reference program's by a relative error of at most 0.0001.
Values sent between devices are 32-bit elements; how exact they have to be, the bound alone decides.
A program may use at most 256 MiB of HBM per device.

```python
import math
import jax
import jax.numpy as jnp
from jax import lax

ORDER = 16384
TILE = 128
PIVOTS = 3
RTD = 16
CTD = 32
N_ROW = 8
N_COL = 4


def draw_matrix(key, part):
    first, second = jax.random.split(jax.random.fold_in(key, 11), 2)
    offdiag = jnp.clip(jax.random.normal(first, (ORDER, ORDER), jnp.float32), -6.0, 6.0)
    heavy = math.sqrt(ORDER) * jax.random.uniform(second, (ORDER,), jnp.float32, 1.0, 2.0)
    indices = jnp.arange(ORDER)
    full = offdiag.at[indices, indices].add(heavy)
    return full.reshape(RTD, N_ROW, TILE, CTD, N_COL, TILE)


def setup_inputs(seed: int = 0) -> dict:
    arg_keys = jax.random.split(jax.random.key(seed), 2)
    return {
        "matrix": draw_matrix(jax.random.fold_in(arg_keys[1], 71), 0),
    }


def newton_inverse(block):
    inv_diag = 1.0 / jnp.diagonal(block)
    return 2.0 * jnp.diag(inv_diag) - inv_diag[:, None] * block * inv_diag[None, :]


def reference(matrix):
    whole = matrix.reshape(ORDER, ORDER)
    for pivot in range(PIVOTS):
        lower = pivot * TILE
        block = whole[lower:lower + TILE, lower:lower + TILE]
        inverse = newton_inverse(block)
        pivot_rows = jnp.dot(inverse, whole[lower:lower + TILE, :], precision=lax.Precision.HIGHEST)
        pivot_rows = pivot_rows.at[:, lower:lower + TILE].set(inverse)
        col_panel = whole[:, lower:lower + TILE]
        zeroed = whole.at[:, lower:lower + TILE].set(jnp.float32(0.0))
        whole = zeroed - jnp.dot(col_panel, pivot_rows, precision=lax.Precision.HIGHEST)
        whole = whole.at[lower:lower + TILE, :].set(pivot_rows)
    return whole.reshape(matrix.shape)
```

```python
import functools

import jax
import jax.numpy as jnp
from jax import lax
from jax.experimental import pallas as pl
from jax.experimental.pallas import tpu as pltpu
from jax.sharding import PartitionSpec as P

PIVOTS = 3
MESH = pl.DeviceIdType.MESH
F32 = jnp.float32
BF16 = jnp.bfloat16


def dot_exact(a, b):
    return jnp.dot(a, b, precision=lax.Precision.HIGHEST, preferred_element_type=F32)


def split(x):
    hi = x.astype(BF16)
    lo = (x - hi.astype(F32)).astype(BF16)
    return hi, lo


def eye_mask(t):
    return lax.broadcasted_iota(jnp.int32, (t, t), 0) == lax.broadcasted_iota(jnp.int32, (t, t), 1)


def newton_inverse(block):
    eye = eye_mask(block.shape[0])
    kept = jnp.where(eye, block, 0.0)
    down = 1.0 / jnp.sum(kept, axis=1, keepdims=True)
    across = 1.0 / jnp.sum(kept, axis=0, keepdims=True)
    return jnp.where(eye, 2.0 * down, 0.0) - down * block * across


def sweep(get, put):
    n = PIVOTS
    a = {(i, j): get(i, j) for i in range(n) for j in range(n)}
    lower, upper = {}, {}
    for p in range(n):
        inverse = newton_inverse(a[p, p])
        rows = {j: inverse if j == p else dot_exact(inverse, a[p, j]) for j in range(n)}
        cols = {i: a[i, p] for i in range(n)}
        for q in range(p + 1):
            lower[p, q] = rows[q]
        for q in range(p):
            upper[q, p] = -cols[q]
        if p + 1 < n:
            for i in range(n):
                if i == p:
                    continue
                for j in range(n):
                    if i < p + 1 and j < p + 1:
                        continue
                    product = dot_exact(cols[i], rows[j])
                    a[i, j] = -product if j == p else a[i, j] - product
            for j in range(n):
                a[p, j] = rows[j]
    for i in range(n):
        for j in range(n):
            total = None
            for s in range(max(i, j), n):
                term = lower[s, j] if s == i else dot_exact(upper[i, s], lower[s, j])
                total = term if total is None else total + term
            put(i, j, total)


def kernel(n_row, n_col, group, blk, mat, out, rows, cols, cells, mix, ccat, rcat,
           load_sem, own_sem, zs_sem, row_recv, col_send, col_recv, cell_send, cell_recv):
    row = lax.axis_index("row")
    col = lax.axis_index("col")
    height, width, t = mat.shape
    n_z = n_row // 2
    n_q = width // group
    z, core = row // 2, lax.rem(row, 2)
    sib = row + 1 - 2 * core
    half = t // 2
    own_half = pl.ds(pl.multiple_of(core * half, half), half)
    other_half = pl.ds(pl.multiple_of((1 - core) * half, half), half)
    out2 = out.reshape(height * width, t)
    rows2 = rows.reshape(PIVOTS * t * width, t)

    loads = [
        pltpu.make_async_copy(
            mat.at[:, pl.ds(q * group, group), :],
            out.at[:, pl.ds(q * group, group), :],
            load_sem.at[q],
        )
        for q in range(n_q)
    ]
    own_rows = pltpu.make_async_copy(mat.at[pl.ds(0, t)], rows.at[jnp.minimum(row, PIVOTS - 1)], own_sem)

    @pl.when(row < PIVOTS)
    def _():
        own_rows.start()

    for load in loads:
        load.start()

    barrier = pltpu.get_barrier_semaphore()
    pl.semaphore_signal(barrier, inc=1, device_id=(sib, col), device_id_type=MESH)

    @pl.when(z > 0)
    def _():
        pl.semaphore_signal(barrier, inc=1, device_id=(row - 2, col), device_id_type=MESH)

    @pl.when(z + 1 < n_z)
    def _():
        pl.semaphore_signal(barrier, inc=1, device_id=(row + 2, col), device_id_type=MESH)

    for d in range(1, n_col):
        pl.semaphore_signal(
            barrier, inc=1, device_id=(row, lax.rem(col + d, n_col)), device_id_type=MESH
        )
    near = jnp.where(z > 0, 1, 0) + jnp.where(z + 1 < n_z, 1, 0)
    pl.semaphore_wait(barrier, n_col + near)

    @pl.when(row < PIVOTS)
    def _():
        own_rows.wait()

    def row_copy(p, q, part, which, kind, target):
        piece = rows.at[p, part, pl.ds(q * group, group), :]
        return pltpu.make_async_remote_copy(
            src_ref=piece,
            dst_ref=piece,
            send_sem=zs_sem.at[p, q, kind],
            recv_sem=row_recv.at[p, q, which],
            device_id=(target, col),
            device_id_type=MESH,
        )

    def row_sends(p, q):
        zp = p // 2
        root = row == p
        return [
            ((z >= zp) & (z + 1 < n_z), row_copy(p, q, own_half, core, 0, row + 2)),
            ((z <= zp) & (z > 0), row_copy(p, q, own_half, core, 1, row - 2)),
            (root, row_copy(p, q, other_half, 1 - core, 2, sib)),
            (root | (z != zp), row_copy(p, q, own_half, core, 3, sib)),
        ]

    def start_sends(p, q):
        for when, copy in row_sends(p, q):
            pl.when(when)(copy.start)

    def root_sends(p, q):
        @pl.when(row == p)
        def _():
            start_sends(p, q)

    def relay(p, q):
        @pl.when(row != p)
        def _():
            row_copy(p, q, own_half, core, 0, sib).wait_recv()
            start_sends(p, q)

    def complete(q):
        for p in range(PIVOTS):
            @pl.when(row != p)
            def _():
                row_copy(p, q, other_half, 1 - core, 0, sib).wait_recv()

    def panel_copy(p, d, part):
        length = height // 2
        piece = cols.at[p, pl.ds(part * length, length), :]
        return pltpu.make_async_remote_copy(
            src_ref=piece,
            dst_ref=piece,
            send_sem=col_send.at[d, part],
            recv_sem=col_recv.at[p, part],
            device_id=(row, lax.rem(col + d, n_col)),
            device_id_type=MESH,
        )

    def cell_copy(p, d):
        return pltpu.make_async_remote_copy(
            src_ref=cells.at[p],
            dst_ref=cells.at[p],
            send_sem=cell_send.at[d],
            recv_sem=cell_recv.at[p],
            device_id=(row, lax.rem(col + d, n_col)),
            device_id_type=MESH,
        )

    def each_root_col(act):
        for p in range(PIVOTS):
            @pl.when(col == p)
            def _():
                act(p)

    def send_panel(part):
        def act(p):
            for d in range(1, n_col):
                panel_copy(p, d, part).start()

        each_root_col(act)

    def wait_panel(part):
        for p in range(PIVOTS):
            @pl.when(col != p)
            def _():
                panel_copy(p, 1, part).wait_recv()

    def take_panel(p):
        @pl.loop(0, height // t)
        def _(b):
            start = pl.multiple_of(b * t, t)
            cols[p, pl.ds(start, t), :] = out2[pl.ds(start * width, t, stride=width), :]

    def send_cells():
        def act(c):
            for p in range(PIVOTS):
                cells[c, pl.ds(p * t, t), :] = rows2[pl.ds(p * t * width, t, stride=width), :]
            for d in range(1, n_col):
                cell_copy(c, d).start()

        each_root_col(act)

    def make_mix():
        for p in range(PIVOTS):
            @pl.when(col != p)
            def _():
                cell_copy(p, 1).wait_recv()

        def put(i, j, value):
            hi, lo = split(value)
            there = pl.ds(j * t, t)
            mix[pl.ds(i * t, t), there] = hi
            mix[pl.ds((PIVOTS + i) * t, t), there] = lo
            mix[pl.ds((2 * PIVOTS + i) * t, t), there] = hi

        sweep(lambda i, j: cells[j, pl.ds(i * t, t), :], put)

    def make_ccat(part):
        eye = jnp.where(eye_mask(t), 1.0, 0.0).astype(F32)
        count = height // t // 2

        @pl.loop(part * count, (part + 1) * count)
        def _(b):
            at = pl.ds(pl.multiple_of(b * t, t), t)
            his, los = [], []
            for p in range(PIVOTS):
                value = cols[p, at, :]
                pivot_rows = (b == 0) & (row < PIVOTS)
                keep = jnp.where(pivot_rows, 0.0, 1.0).astype(F32)
                unit = jnp.where(pivot_rows & (row == p), -1.0, 0.0).astype(F32)
                hi, lo = split(value * keep + eye * unit)
                his.append(hi)
                los.append(lo)
            left = jnp.concatenate(his + his + los, axis=1)
            hi, lo = split(jnp.dot(left, mix[...], preferred_element_type=F32))
            wide = PIVOTS * t
            ccat[at, pl.ds(0, wide)] = hi
            ccat[at, pl.ds(wide, wide)] = hi
            ccat[at, pl.ds(2 * wide, wide)] = lo

    def make_rcat(q):
        eye = jnp.where(eye_mask(t), 1.0, 0.0).astype(F32)
        for j in range(group):
            there = pl.ds(j * t, t)
            for p in range(PIVOTS):
                value = rows2[pl.ds(p * t * width + q * group + j, t, stride=width), :]
                if q == 0 and j == 0:
                    keep = jnp.where(col < PIVOTS, 0.0, 1.0).astype(F32)
                    unit = jnp.where(col == p, 1.0, 0.0).astype(F32)
                    value = value * keep + eye * unit
                hi, lo = split(value)
                rcat[pl.ds(p * t, t), there] = hi
                rcat[pl.ds((PIVOTS + p) * t, t), there] = lo
                rcat[pl.ds((2 * PIVOTS + p) * t, t), there] = hi

    def update(q, first, last):
        n_blk = height // blk

        @pl.loop(n_blk * first // 4, n_blk * last // 4)
        def _(b):
            start = pl.multiple_of(b * blk, blk)
            product = jnp.dot(ccat[pl.ds(start, blk), :], rcat[...], preferred_element_type=F32)
            for j in range(group):
                at = pl.ds(start * width + q * group + j, blk, stride=width)
                out2[at, :] = out2[at, :] - product[:, j * t : (j + 1) * t]

    def clear_base():
        @pl.when(row < PIVOTS)
        def _():
            @pl.loop(0, t)
            def _(i):
                out[i] = jnp.zeros((width, t), F32)

        @pl.when(col < PIVOTS)
        def _():
            @pl.loop(0, height // t)
            def _(b):
                start = pl.multiple_of(b * t, t)
                out2[pl.ds(start * width, t, stride=width), :] = jnp.zeros((t, t), F32)

    order = list(reversed(range(PIVOTS)))
    for p in order:
        root_sends(p, 0)
    loads[0].wait()
    each_root_col(take_panel)
    send_panel(0)
    work = []
    for q in range(n_q):
        for p in order:
            if q > 0:
                root_sends(p, q)
            relay(p, q)
            if work and q > 0:
                work.pop(0)()
        complete(q)
        if q == 0:
            send_cells()
            send_panel(1)

            def base():
                for load in loads[1:]:
                    load.wait()
                clear_base()

            def left():
                wait_panel(0)
                make_ccat(0)

            def rest():
                wait_panel(1)
                make_ccat(1)

            work += [base, lambda: None, lambda: None, make_mix, left, rest]
        parts = 4 if q == n_q - 1 else 2
        if q == 0:
            parts = 2
        for k in range(parts):
            def some(q=q, k=k, parts=parts):
                if k == 0:
                    make_rcat(q)
                update(q, 4 * k // parts, 4 * (k + 1) // parts)

            work.append(some)
    for act in work:
        act()

    for q in range(n_q):
        for p in range(PIVOTS):
            for when, copy in row_sends(p, q):
                pl.when(when)(copy.wait_send)

    def drain(p):
        for d in range(1, n_col):
            panel_copy(p, d, 0).wait_send()
            panel_copy(p, d, 1).wait_send()
            cell_copy(p, d).wait_send()

    each_root_col(drain)


def local(matrix):
    n_row = lax.axis_size("row")
    n_col = lax.axis_size("col")
    row_tiles, _, t, col_tiles, _, _ = matrix.shape
    height = row_tiles * t
    assert n_row % 2 == 0 and PIVOTS <= min(n_row, n_col)
    group = min(8, col_tiles)
    n_q = col_tiles // group
    blk = min(256, height // 4)
    flat = matrix.reshape(height, col_tiles, t)
    wide = PIVOTS * t
    result = pl.pallas_call(
        functools.partial(kernel, n_row, n_col, group, blk),
        out_shape=OUT(flat.shape, F32),
        in_specs=[pl.BlockSpec(memory_space=pl.ANY)],
        out_specs=pl.BlockSpec(memory_space=OUT_SPACE),
        scratch_shapes=[
            pltpu.VMEM((PIVOTS, t, col_tiles, t), F32),
            pltpu.VMEM((PIVOTS, height, t), F32),
            pltpu.VMEM((PIVOTS, wide, t), F32),
            pltpu.VMEM((3 * wide, wide), BF16),
            pltpu.VMEM((height, 3 * wide), BF16),
            pltpu.VMEM((3 * wide, group * t), BF16),
            pltpu.SemaphoreType.DMA((n_q,)),
            pltpu.SemaphoreType.DMA,
            pltpu.SemaphoreType.DMA((PIVOTS, n_q, 4)),
            pltpu.SemaphoreType.DMA((PIVOTS, n_q, 2)),
            pltpu.SemaphoreType.DMA((n_col, 2)),
            pltpu.SemaphoreType.DMA((PIVOTS, 2)),
            pltpu.SemaphoreType.DMA((n_col,)),
            pltpu.SemaphoreType.DMA((PIVOTS,)),
        ],
        compiler_params=pltpu.CompilerParams(
            collective_id=0, has_side_effects=True, vmem_limit_bytes=VMEM_LIMIT
        ),
        cost_estimate=pl.CostEstimate(
            flops=6 * height * wide * col_tiles * t,
            bytes_accessed=8 * height * col_tiles * t,
            transcendentals=0,
        ),
    )(flat)
    return result.reshape(matrix.shape)


OUT = pltpu.VMEM
OUT_SPACE = pltpu.VMEM
VMEM_LIMIT = 26 * 2**20


def solution(mesh):
    in_specs = (P(None, "row", None, None, "col", None),)
    out_specs = P(None, "row", None, None, "col", None)
    return jax.shard_map(local, mesh=mesh, in_specs=in_specs, out_specs=out_specs, check_vma=False)
```

```python
import functools

import jax
import jax.numpy as jnp
from jax import lax
from jax.experimental import pallas as pl
from jax.experimental.pallas import tpu as pltpu
from jax.sharding import PartitionSpec as P

PIVOTS = 3
MESH = pl.DeviceIdType.MESH
F32 = jnp.float32
BF16 = jnp.bfloat16


def dot_exact(a, b):
    return jnp.dot(a, b, precision=lax.Precision.HIGHEST, preferred_element_type=F32)


def split(x):
    hi = x.astype(BF16)
    lo = (x - hi.astype(F32)).astype(BF16)
    return hi, lo


def eye_mask(t):
    return lax.broadcasted_iota(jnp.int32, (t, t), 0) == lax.broadcasted_iota(jnp.int32, (t, t), 1)


def turn(tiles):
    tiles = list(tiles)
    place = lax.broadcasted_iota(jnp.int32, tiles[0].shape, 1)
    for k in (1, 2, 4):
        low = (place // k) % 2 == 0
        for j in range(8):
            if (j // k) % 2:
                continue
            a, b = tiles[j], tiles[j + k]
            tiles[j] = jnp.where(low, a, pltpu.roll(b, k, 1))
            tiles[j + k] = jnp.where(low, pltpu.roll(a, 8 - k, 1), b)
    return tiles


def newton_inverse(block):
    eye = eye_mask(block.shape[0])
    kept = jnp.where(eye, block, 0.0)
    down = 1.0 / jnp.sum(kept, axis=1, keepdims=True)
    across = 1.0 / jnp.sum(kept, axis=0, keepdims=True)
    return jnp.where(eye, 2.0 * down, 0.0) - down * block * across


def sweep(get, put):
    n = PIVOTS
    a = {(i, j): get(i, j) for i in range(n) for j in range(n)}
    lower, upper = {}, {}
    for p in range(n):
        inverse = newton_inverse(a[p, p])
        rows = {j: inverse if j == p else dot_exact(inverse, a[p, j]) for j in range(n)}
        cols = {i: a[i, p] for i in range(n)}
        for q in range(p + 1):
            lower[p, q] = rows[q]
        for q in range(p):
            upper[q, p] = -cols[q]
        if p + 1 < n:
            for i in range(n):
                if i == p:
                    continue
                for j in range(n):
                    if i < p + 1 and j < p + 1:
                        continue
                    product = dot_exact(cols[i], rows[j])
                    a[i, j] = -product if j == p else a[i, j] - product
            for j in range(n):
                a[p, j] = rows[j]
    for i in range(n):
        for j in range(n):
            total = None
            for s in range(max(i, j), n):
                term = lower[s, j] if s == i else dot_exact(upper[i, s], lower[s, j])
                total = term if total is None else total + term
            put(i, j, total)


def kernel(n_row, n_col, group, blk, mat, out, rows, cols, cells, mix, ccat, rcat,
           load_sem, own_sem, zs_sem, row_recv, col_send, col_recv, cell_send, cell_recv):
    row = lax.axis_index("row")
    col = lax.axis_index("col")
    height, width, t = mat.shape
    n_z = n_row // 2
    n_q = width // group
    z, core = row // 2, lax.rem(row, 2)
    sib = row + 1 - 2 * core
    half = t // 2
    own_half = pl.ds(pl.multiple_of(core * half, half), half)
    other_half = pl.ds(pl.multiple_of((1 - core) * half, half), half)
    out2 = out.reshape(height * width, t)
    out8 = out.reshape(height // 8, 8, width, t)
    step = 32
    rows2 = rows.reshape(PIVOTS * t * width, t)

    loads = [
        pltpu.make_async_copy(
            mat.at[:, pl.ds(q * group, group), :],
            out.at[:, pl.ds(q * group, group), :],
            load_sem.at[q],
        )
        for q in range(n_q)
    ]
    own_rows = pltpu.make_async_copy(mat.at[pl.ds(0, t)], rows.at[jnp.minimum(row, PIVOTS - 1)], own_sem)

    @pl.when(row < PIVOTS)
    def _():
        own_rows.start()

    for load in loads:
        load.start()

    barrier = pltpu.get_barrier_semaphore()
    pl.semaphore_signal(barrier, inc=1, device_id=(sib, col), device_id_type=MESH)

    @pl.when(z > 0)
    def _():
        pl.semaphore_signal(barrier, inc=1, device_id=(row - 2, col), device_id_type=MESH)

    @pl.when(z + 1 < n_z)
    def _():
        pl.semaphore_signal(barrier, inc=1, device_id=(row + 2, col), device_id_type=MESH)

    for d in range(1, n_col):
        pl.semaphore_signal(
            barrier, inc=1, device_id=(row, lax.rem(col + d, n_col)), device_id_type=MESH
        )
    near = jnp.where(z > 0, 1, 0) + jnp.where(z + 1 < n_z, 1, 0)
    pl.semaphore_wait(barrier, n_col + near)

    @pl.when(row < PIVOTS)
    def _():
        own_rows.wait()

    def row_copy(p, q, part, which, kind, target):
        piece = rows.at[p, part, pl.ds(q * group, group), :]
        return pltpu.make_async_remote_copy(
            src_ref=piece,
            dst_ref=piece,
            send_sem=zs_sem.at[p, q, kind],
            recv_sem=row_recv.at[p, q, which],
            device_id=(target, col),
            device_id_type=MESH,
        )

    def row_sends(p, q):
        zp = p // 2
        root = row == p
        return [
            ((z >= zp) & (z + 1 < n_z), row_copy(p, q, own_half, core, 0, row + 2)),
            ((z <= zp) & (z > 0), row_copy(p, q, own_half, core, 1, row - 2)),
            (root, row_copy(p, q, other_half, 1 - core, 2, sib)),
            (root | (z != zp), row_copy(p, q, own_half, core, 3, sib)),
        ]

    def start_sends(p, q):
        for when, copy in row_sends(p, q):
            pl.when(when)(copy.start)

    def root_sends(p, q):
        @pl.when(row == p)
        def _():
            start_sends(p, q)

    def relay(p, q):
        @pl.when(row != p)
        def _():
            row_copy(p, q, own_half, core, 0, sib).wait_recv()
            start_sends(p, q)

    def complete(q):
        for p in range(PIVOTS):
            @pl.when(row != p)
            def _():
                row_copy(p, q, other_half, 1 - core, 0, sib).wait_recv()

    def panel_copy(p, d, part):
        length = height // 2
        piece = cols.at[p, pl.ds(part * length, length), :]
        return pltpu.make_async_remote_copy(
            src_ref=piece,
            dst_ref=piece,
            send_sem=col_send.at[d, part],
            recv_sem=col_recv.at[p, part],
            device_id=(row, lax.rem(col + d, n_col)),
            device_id_type=MESH,
        )

    def cell_copy(p, d):
        return pltpu.make_async_remote_copy(
            src_ref=cells.at[p],
            dst_ref=cells.at[p],
            send_sem=cell_send.at[d],
            recv_sem=cell_recv.at[p],
            device_id=(row, lax.rem(col + d, n_col)),
            device_id_type=MESH,
        )

    def each_root_col(act):
        for p in range(PIVOTS):
            @pl.when(col == p)
            def _():
                act(p)

    def send_panel(part):
        def act(p):
            for d in range(1, n_col):
                panel_copy(p, d, part).start()

        each_root_col(act)

    def wait_panel(part):
        for p in range(PIVOTS):
            @pl.when(col != p)
            def _():
                panel_copy(p, 1, part).wait_recv()

    def take_panel(p):
        @pl.loop(0, height // t)
        def _(b):
            start = pl.multiple_of(b * t, t)
            cols[p, pl.ds(start, t), :] = out2[pl.ds(start * width, t, stride=width), :]

    def send_cells():
        def act(c):
            for p in range(PIVOTS):
                cells[c, pl.ds(p * t, t), :] = rows2[pl.ds(p * t * width, t, stride=width), :]
            for d in range(1, n_col):
                cell_copy(c, d).start()

        each_root_col(act)

    def make_mix():
        for p in range(PIVOTS):
            @pl.when(col != p)
            def _():
                cell_copy(p, 1).wait_recv()

        def put(i, j, value):
            hi, lo = split(value)
            there = pl.ds(j * t, t)
            mix[pl.ds(i * t, t), there] = hi
            mix[pl.ds((PIVOTS + i) * t, t), there] = lo
            mix[pl.ds((2 * PIVOTS + i) * t, t), there] = hi

        sweep(lambda i, j: cells[j, pl.ds(i * t, t), :], put)

    def make_ccat(part):
        eye = jnp.where(eye_mask(t), 1.0, 0.0).astype(F32)
        count = height // t // 2

        @pl.loop(part * count, (part + 1) * count)
        def _(b):
            at = pl.ds(pl.multiple_of(b * t, t), t)
            his, los = [], []
            for p in range(PIVOTS):
                value = cols[p, at, :]
                pivot_rows = (b == 0) & (row < PIVOTS)
                keep = jnp.where(pivot_rows, 0.0, 1.0).astype(F32)
                unit = jnp.where(pivot_rows & (row == p), -1.0, 0.0).astype(F32)
                hi, lo = split(value * keep + eye * unit)
                his.append(hi)
                los.append(lo)
            left = jnp.concatenate(his + his + los, axis=1)
            hi, lo = split(jnp.dot(left, mix[...], preferred_element_type=F32))
            wide = PIVOTS * t
            ccat[at, pl.ds(0, wide)] = hi
            ccat[at, pl.ds(wide, wide)] = hi
            ccat[at, pl.ds(2 * wide, wide)] = lo

    def make_rcat(q):
        eye = jnp.where(eye_mask(t), 1.0, 0.0).astype(F32)
        for j in range(group):
            there = pl.ds(j * t, t)
            for p in range(PIVOTS):
                value = rows2[pl.ds(p * t * width + q * group + j, t, stride=width), :]
                if q == 0 and j == 0:
                    keep = jnp.where(col < PIVOTS, 0.0, 1.0).astype(F32)
                    unit = jnp.where(col == p, 1.0, 0.0).astype(F32)
                    value = value * keep + eye * unit
                hi, lo = split(value)
                rcat[pl.ds(p * t, t), there] = hi
                rcat[pl.ds((PIVOTS + p) * t, t), there] = lo
                rcat[pl.ds((2 * PIVOTS + p) * t, t), there] = hi

    def update(q, first, last):
        n_blk = height // blk

        @pl.loop(n_blk * first // 4, n_blk * last // 4)
        def _(b):
            start = pl.multiple_of(b * blk, blk)
            product = jnp.dot(ccat[pl.ds(start, blk), :], rcat[...], preferred_element_type=F32)
            for k in range(blk // step):
                part = product[k * step : (k + 1) * step]
                tiles = [part[:, j * t : (j + 1) * t].reshape(step // 8, 8, t) for j in range(group)]
                above = pl.multiple_of(start // 8 + k * (step // 8), step // 8)
                for i, tile in enumerate(turn(tiles)):
                    at = (pl.ds(above, step // 8), i, pl.ds(q * group, group), slice(None))
                    out8[at] = out8[at] - tile

    def clear_base():
        @pl.when(row < PIVOTS)
        def _():
            @pl.loop(0, t)
            def _(i):
                out[i] = jnp.zeros((width, t), F32)

        @pl.when(col < PIVOTS)
        def _():
            @pl.loop(0, height // t)
            def _(b):
                start = pl.multiple_of(b * t, t)
                out2[pl.ds(start * width, t, stride=width), :] = jnp.zeros((t, t), F32)

    order = list(reversed(range(PIVOTS)))
    for q in range(n_q):
        for p in order:
            if p < 2 or q < 2:
                root_sends(p, q)
    loads[0].wait()
    each_root_col(take_panel)
    send_panel(0)
    work = []
    for q in range(n_q):
        for p in order:
            if q == 0 or p >= 2:
                relay(p, q)
            else:
                @pl.when(z != 0)
                def _():
                    relay(p, q)
            if work and q > 0:
                work.pop(0)()
        complete(q)
        if q + 2 < n_q:
            for p in order:
                if p >= 2:
                    root_sends(p, q + 2)
        if q == 0:
            send_cells()
            send_panel(1)

            @pl.when(z == 0)
            def _():
                for later in range(1, n_q):
                    for p in order:
                        if p < 2:
                            relay(p, later)

            def base():
                for load in loads[1:]:
                    load.wait()
                clear_base()

            def left():
                wait_panel(0)
                make_ccat(0)

            def rest():
                wait_panel(1)
                make_ccat(1)

            work += [base, lambda: None, lambda: None, make_mix, left, rest]
        parts = 4 if q == n_q - 1 else 2
        if q == 0:
            parts = 2
        for k in range(parts):
            def some(q=q, k=k, parts=parts):
                if k == 0:
                    make_rcat(q)
                update(q, 4 * k // parts, 4 * (k + 1) // parts)

            work.append(some)
    for act in work:
        act()

    for q in range(n_q):
        for p in range(PIVOTS):
            for when, copy in row_sends(p, q):
                pl.when(when)(copy.wait_send)

    def drain(p):
        for d in range(1, n_col):
            panel_copy(p, d, 0).wait_send()
            panel_copy(p, d, 1).wait_send()
            cell_copy(p, d).wait_send()

    each_root_col(drain)


def local(matrix):
    n_row = lax.axis_size("row")
    n_col = lax.axis_size("col")
    row_tiles, _, t, col_tiles, _, _ = matrix.shape
    height = row_tiles * t
    assert n_row % 2 == 0 and PIVOTS <= min(n_row, n_col)
    group = 8
    assert col_tiles % group == 0 and t % 32 == 0
    n_q = col_tiles // group
    blk = min(256, height // 4)
    flat = matrix.reshape(height, col_tiles, t)
    wide = PIVOTS * t
    result = pl.pallas_call(
        functools.partial(kernel, n_row, n_col, group, blk),
        out_shape=OUT(flat.shape, F32),
        in_specs=[pl.BlockSpec(memory_space=pl.ANY)],
        out_specs=pl.BlockSpec(memory_space=OUT_SPACE),
        scratch_shapes=[
            pltpu.VMEM((PIVOTS, t, col_tiles, t), F32),
            pltpu.VMEM((PIVOTS, height, t), F32),
            pltpu.VMEM((PIVOTS, wide, t), F32),
            pltpu.VMEM((3 * wide, wide), BF16),
            pltpu.VMEM((height, 3 * wide), BF16),
            pltpu.VMEM((3 * wide, group * t), BF16),
            pltpu.SemaphoreType.DMA((n_q,)),
            pltpu.SemaphoreType.DMA,
            pltpu.SemaphoreType.DMA((PIVOTS, n_q, 4)),
            pltpu.SemaphoreType.DMA((PIVOTS, n_q, 2)),
            pltpu.SemaphoreType.DMA((n_col, 2)),
            pltpu.SemaphoreType.DMA((PIVOTS, 2)),
            pltpu.SemaphoreType.DMA((n_col,)),
            pltpu.SemaphoreType.DMA((PIVOTS,)),
        ],
        compiler_params=pltpu.CompilerParams(
            collective_id=0, has_side_effects=True, vmem_limit_bytes=VMEM_LIMIT
        ),
        cost_estimate=pl.CostEstimate(
            flops=6 * height * wide * col_tiles * t,
            bytes_accessed=8 * height * col_tiles * t,
            transcendentals=0,
        ),
    )(flat)
    return result.reshape(matrix.shape)


OUT = pltpu.VMEM
OUT_SPACE = pltpu.VMEM
VMEM_LIMIT = 26 * 2**20


def solution(mesh):
    in_specs = (P(None, "row", None, None, "col", None),)
    out_specs = P(None, "row", None, None, "col", None)
    return jax.shard_map(local, mesh=mesh, in_specs=in_specs, out_specs=out_specs, check_vma=False)
```

```python
import functools

import jax
import jax.numpy as jnp
from jax import lax
from jax.experimental import pallas as pl
from jax.experimental.pallas import tpu as pltpu
from jax.sharding import PartitionSpec as P

PIVOTS = 3
MESH = pl.DeviceIdType.MESH
F32 = jnp.float32
BF16 = jnp.bfloat16


def dot_exact(a, b):
    return jnp.dot(a, b, precision=lax.Precision.HIGHEST, preferred_element_type=F32)


def split(x):
    hi = x.astype(BF16)
    lo = (x - hi.astype(F32)).astype(BF16)
    return hi, lo


def eye_mask(t):
    return lax.broadcasted_iota(jnp.int32, (t, t), 0) == lax.broadcasted_iota(jnp.int32, (t, t), 1)


def turn(tiles):
    tiles = list(tiles)
    place = lax.broadcasted_iota(jnp.int32, tiles[0].shape, 1)
    for k in (1, 2, 4):
        low = (place // k) % 2 == 0
        for j in range(8):
            if (j // k) % 2:
                continue
            a, b = tiles[j], tiles[j + k]
            tiles[j] = jnp.where(low, a, pltpu.roll(b, k, 1))
            tiles[j + k] = jnp.where(low, pltpu.roll(a, 8 - k, 1), b)
    return tiles


def newton_inverse(block):
    eye = eye_mask(block.shape[0])
    kept = jnp.where(eye, block, 0.0)
    down = 1.0 / jnp.sum(kept, axis=1, keepdims=True)
    across = 1.0 / jnp.sum(kept, axis=0, keepdims=True)
    return jnp.where(eye, 2.0 * down, 0.0) - down * block * across


def sweep(get, put):
    n = PIVOTS
    a = {(i, j): get(i, j) for i in range(n) for j in range(n)}
    lower, upper = {}, {}
    for p in range(n):
        inverse = newton_inverse(a[p, p])
        rows = {j: inverse if j == p else dot_exact(inverse, a[p, j]) for j in range(n)}
        cols = {i: a[i, p] for i in range(n)}
        for q in range(p + 1):
            lower[p, q] = rows[q]
        for q in range(p):
            upper[q, p] = -cols[q]
        if p + 1 < n:
            for i in range(n):
                if i == p:
                    continue
                for j in range(n):
                    if i < p + 1 and j < p + 1:
                        continue
                    product = dot_exact(cols[i], rows[j])
                    a[i, j] = -product if j == p else a[i, j] - product
            for j in range(n):
                a[p, j] = rows[j]
    for i in range(n):
        for j in range(n):
            total = None
            for s in range(max(i, j), n):
                term = lower[s, j] if s == i else dot_exact(upper[i, s], lower[s, j])
                total = term if total is None else total + term
            put(i, j, total)


def kernel(n_row, n_col, group, blk, mat, out, rows, cols, cells, mix, ccat, rcat,
           load_sem, own_sem, zs_sem, row_recv, col_send, col_recv, cell_send, cell_recv):
    row = lax.axis_index("row")
    col = lax.axis_index("col")
    height, width, t = mat.shape
    n_z = n_row // 2
    n_q = width // group
    z, core = row // 2, lax.rem(row, 2)
    sib = row + 1 - 2 * core
    half = t // 2
    own_half = pl.ds(pl.multiple_of(core * half, half), half)
    other_half = pl.ds(pl.multiple_of((1 - core) * half, half), half)
    out2 = out.reshape(height * width, t)
    out8 = out.reshape(height // 8, 8, width, t)
    step = 32
    rows2 = rows.reshape(PIVOTS * t * width, t)

    loads = [
        pltpu.make_async_copy(
            mat.at[:, pl.ds(q * group, group), :],
            out.at[:, pl.ds(q * group, group), :],
            load_sem.at[q],
        )
        for q in range(n_q)
    ]
    own_rows = pltpu.make_async_copy(mat.at[pl.ds(0, t)], rows.at[jnp.minimum(row, PIVOTS - 1)], own_sem)

    @pl.when(row < PIVOTS)
    def _():
        own_rows.start()

    for load in loads:
        load.start()

    barrier = pltpu.get_barrier_semaphore()
    pl.semaphore_signal(barrier, inc=1, device_id=(sib, col), device_id_type=MESH)

    @pl.when(z > 0)
    def _():
        pl.semaphore_signal(barrier, inc=1, device_id=(row - 2, col), device_id_type=MESH)

    @pl.when(z + 1 < n_z)
    def _():
        pl.semaphore_signal(barrier, inc=1, device_id=(row + 2, col), device_id_type=MESH)

    for d in range(1, n_col):
        pl.semaphore_signal(
            barrier, inc=1, device_id=(row, lax.rem(col + d, n_col)), device_id_type=MESH
        )
    near = jnp.where(z > 0, 1, 0) + jnp.where(z + 1 < n_z, 1, 0)
    pl.semaphore_wait(barrier, n_col + near)

    @pl.when(row < PIVOTS)
    def _():
        own_rows.wait()

    def row_copy(p, q, part, which, kind, target):
        piece = rows.at[p, part, pl.ds(q * group, group), :]
        return pltpu.make_async_remote_copy(
            src_ref=piece,
            dst_ref=piece,
            send_sem=zs_sem.at[p, q, kind],
            recv_sem=row_recv.at[p, q, which],
            device_id=(target, col),
            device_id_type=MESH,
        )

    def row_sends(p, q):
        zp = p // 2
        root = row == p
        return [
            ((z >= zp) & (z + 1 < n_z), row_copy(p, q, own_half, core, 0, row + 2)),
            ((z <= zp) & (z > 0), row_copy(p, q, own_half, core, 1, row - 2)),
            (root, row_copy(p, q, other_half, 1 - core, 2, sib)),
            (root | (z != zp), row_copy(p, q, own_half, core, 3, sib)),
        ]

    def start_sends(p, q):
        for when, copy in row_sends(p, q):
            pl.when(when)(copy.start)

    def root_sends(p, q):
        @pl.when(row == p)
        def _():
            start_sends(p, q)

    def relay(p, q):
        @pl.when(row != p)
        def _():
            row_copy(p, q, own_half, core, 0, sib).wait_recv()
            start_sends(p, q)

    def complete(q):
        for p in range(PIVOTS):
            @pl.when(row != p)
            def _():
                row_copy(p, q, other_half, 1 - core, 0, sib).wait_recv()

    def panel_copy(p, d, part):
        length = height // 2
        piece = cols.at[p, pl.ds(part * length, length), :]
        return pltpu.make_async_remote_copy(
            src_ref=piece,
            dst_ref=piece,
            send_sem=col_send.at[d, part],
            recv_sem=col_recv.at[p, part],
            device_id=(row, lax.rem(col + d, n_col)),
            device_id_type=MESH,
        )

    def cell_copy(p, d):
        return pltpu.make_async_remote_copy(
            src_ref=cells.at[p],
            dst_ref=cells.at[p],
            send_sem=cell_send.at[d],
            recv_sem=cell_recv.at[p],
            device_id=(row, lax.rem(col + d, n_col)),
            device_id_type=MESH,
        )

    def each_root_col(act):
        for p in range(PIVOTS):
            @pl.when(col == p)
            def _():
                act(p)

    def send_panel(part):
        def act(p):
            for d in range(1, n_col):
                panel_copy(p, d, part).start()

        each_root_col(act)

    def wait_panel(part):
        for p in range(PIVOTS):
            @pl.when(col != p)
            def _():
                panel_copy(p, 1, part).wait_recv()

    def take_panel(p):
        @pl.loop(0, height // t)
        def _(b):
            start = pl.multiple_of(b * t, t)
            cols[p, pl.ds(start, t), :] = out2[pl.ds(start * width, t, stride=width), :]

    def send_cells():
        def act(c):
            for p in range(PIVOTS):
                cells[c, pl.ds(p * t, t), :] = rows2[pl.ds(p * t * width, t, stride=width), :]
            for d in range(1, n_col):
                cell_copy(c, d).start()

        each_root_col(act)

    def make_mix():
        for p in range(PIVOTS):
            @pl.when(col != p)
            def _():
                cell_copy(p, 1).wait_recv()

        def put(i, j, value):
            hi, lo = split(value)
            there = pl.ds(j * t, t)
            mix[pl.ds(i * t, t), there] = hi
            mix[pl.ds((PIVOTS + i) * t, t), there] = lo
            mix[pl.ds((2 * PIVOTS + i) * t, t), there] = hi

        sweep(lambda i, j: cells[j, pl.ds(i * t, t), :], put)

    def make_ccat(part):
        eye = jnp.where(eye_mask(t), 1.0, 0.0).astype(F32)
        count = height // t // 2

        @pl.loop(part * count, (part + 1) * count)
        def _(b):
            at = pl.ds(pl.multiple_of(b * t, t), t)
            his, los = [], []
            for p in range(PIVOTS):
                value = cols[p, at, :]
                pivot_rows = (b == 0) & (row < PIVOTS)
                keep = jnp.where(pivot_rows, 0.0, 1.0).astype(F32)
                unit = jnp.where(pivot_rows & (row == p), -1.0, 0.0).astype(F32)
                hi, lo = split(value * keep + eye * unit)
                his.append(hi)
                los.append(lo)
            left = jnp.concatenate(his + his + los, axis=1)
            hi, lo = split(jnp.dot(left, mix[...], preferred_element_type=F32))
            wide = PIVOTS * t
            ccat[at, pl.ds(0, wide)] = hi
            ccat[at, pl.ds(wide, wide)] = hi
            ccat[at, pl.ds(2 * wide, wide)] = lo

    def make_rcat(q):
        eye = jnp.where(eye_mask(t), 1.0, 0.0).astype(F32)
        for j in range(group):
            there = pl.ds(j * t, t)
            for p in range(PIVOTS):
                value = rows2[pl.ds(p * t * width + q * group + j, t, stride=width), :]
                if q == 0 and j == 0:
                    keep = jnp.where(col < PIVOTS, 0.0, 1.0).astype(F32)
                    unit = jnp.where(col == p, 1.0, 0.0).astype(F32)
                    value = value * keep + eye * unit
                hi, lo = split(value)
                rcat[pl.ds(p * t, t), there] = hi
                rcat[pl.ds((PIVOTS + p) * t, t), there] = lo
                rcat[pl.ds((2 * PIVOTS + p) * t, t), there] = hi

    def update(q, first, last):
        n_blk = height // blk

        @pl.loop(n_blk * first // 4, n_blk * last // 4)
        def _(b):
            start = pl.multiple_of(b * blk, blk)
            product = jnp.dot(ccat[pl.ds(start, blk), :], rcat[...], preferred_element_type=F32)
            for k in range(blk // step):
                part = product[k * step : (k + 1) * step]
                tiles = [part[:, j * t : (j + 1) * t].reshape(step // 8, 8, t) for j in range(group)]
                above = pl.multiple_of(start // 8 + k * (step // 8), step // 8)
                for i, tile in enumerate(turn(tiles)):
                    at = (pl.ds(above, step // 8), i, pl.ds(q * group, group), slice(None))
                    out8[at] = out8[at] - tile

    def clear_base():
        @pl.when(row < PIVOTS)
        def _():
            @pl.loop(0, t)
            def _(i):
                out[i] = jnp.zeros((width, t), F32)

        @pl.when(col < PIVOTS)
        def _():
            @pl.loop(0, height // t)
            def _(b):
                start = pl.multiple_of(b * t, t)
                out2[pl.ds(start * width, t, stride=width), :] = jnp.zeros((t, t), F32)

    order = list(reversed(range(PIVOTS)))
    for q in range(n_q):
        for p in order:
            if p < 2 or q < 2:
                root_sends(p, q)
    loads[0].wait()
    each_root_col(take_panel)
    send_panel(0)
    ready, work = [], []
    for q in range(n_q):
        for p in order:
            if q == 0 or p >= 2:
                relay(p, q)
            else:
                @pl.when(z != 0)
                def _():
                    relay(p, q)
        complete(q)
        if q == n_q - 2:
            for act in ready:
                act()
            ready = []
        if q + 2 < n_q:
            for p in order:
                if p >= 2:
                    root_sends(p, q + 2)
        if q == 0:
            send_cells()
            send_panel(1)

            @pl.when(z == 0)
            def _():
                for later in range(1, n_q):
                    for p in order:
                        if p < 2:
                            relay(p, later)

            def base():
                for load in loads[1:]:
                    load.wait()
                clear_base()

            def left():
                wait_panel(0)
                make_ccat(0)

            def rest():
                wait_panel(1)
                make_ccat(1)

            ready = [base, make_mix, left, rest]

        def some(q=q):
            make_rcat(q)
            update(q, 0, 4)

        work.append(some)
    for act in ready + work:
        act()

    for q in range(n_q):
        for p in range(PIVOTS):
            for when, copy in row_sends(p, q):
                pl.when(when)(copy.wait_send)

    def drain(p):
        for d in range(1, n_col):
            panel_copy(p, d, 0).wait_send()
            panel_copy(p, d, 1).wait_send()
            cell_copy(p, d).wait_send()

    each_root_col(drain)


def local(matrix):
    n_row = lax.axis_size("row")
    n_col = lax.axis_size("col")
    row_tiles, _, t, col_tiles, _, _ = matrix.shape
    height = row_tiles * t
    assert n_row % 2 == 0 and PIVOTS <= min(n_row, n_col)
    group = 8
    assert col_tiles % group == 0 and t % 32 == 0
    n_q = col_tiles // group
    blk = min(256, height // 4)
    flat = matrix.reshape(height, col_tiles, t)
    wide = PIVOTS * t
    result = pl.pallas_call(
        functools.partial(kernel, n_row, n_col, group, blk),
        out_shape=OUT(flat.shape, F32),
        in_specs=[pl.BlockSpec(memory_space=pl.ANY)],
        out_specs=pl.BlockSpec(memory_space=OUT_SPACE),
        scratch_shapes=[
            pltpu.VMEM((PIVOTS, t, col_tiles, t), F32),
            pltpu.VMEM((PIVOTS, height, t), F32),
            pltpu.VMEM((PIVOTS, wide, t), F32),
            pltpu.VMEM((3 * wide, wide), BF16),
            pltpu.VMEM((height, 3 * wide), BF16),
            pltpu.VMEM((3 * wide, group * t), BF16),
            pltpu.SemaphoreType.DMA((n_q,)),
            pltpu.SemaphoreType.DMA,
            pltpu.SemaphoreType.DMA((PIVOTS, n_q, 4)),
            pltpu.SemaphoreType.DMA((PIVOTS, n_q, 2)),
            pltpu.SemaphoreType.DMA((n_col, 2)),
            pltpu.SemaphoreType.DMA((PIVOTS, 2)),
            pltpu.SemaphoreType.DMA((n_col,)),
            pltpu.SemaphoreType.DMA((PIVOTS,)),
        ],
        compiler_params=pltpu.CompilerParams(
            collective_id=0, has_side_effects=True, vmem_limit_bytes=VMEM_LIMIT
        ),
        cost_estimate=pl.CostEstimate(
            flops=6 * height * wide * col_tiles * t,
            bytes_accessed=8 * height * col_tiles * t,
            transcendentals=0,
        ),
    )(flat)
    return result.reshape(matrix.shape)


OUT = pltpu.VMEM
OUT_SPACE = pltpu.VMEM
VMEM_LIMIT = 26 * 2**20


def solution(mesh):
    in_specs = (P(None, "row", None, None, "col", None),)
    out_specs = P(None, "row", None, None, "col", None)
    return jax.shard_map(local, mesh=mesh, in_specs=in_specs, out_specs=out_specs, check_vma=False)
```
